32 devices in a mesh: row: 4 (over z), col: 8 (over y, x, core).
Axes of the slice: x: 2, y: 2, z: 4, core: 2. Of those that a mesh axis runs over, the one named last changes fastest.
Arguments:
- tokens: bfloat16 [512, 6144], P('row', 'col'), may hold values from -6 to 6
- weight: bfloat16 [6144, 24576], P('row', 'col'), may hold values from -0.078125 to 0.078125
- act_grad: bfloat16 [512, 24576], P('row', 'col'), may hold values from -6 to 6
Outputs:
- activation: bfloat16 [512, 24576], P('row', 'col')
- input_grad: bfloat16 [512, 6144], P('col', 'row')
- weight_grad: bfloat16 [6144, 24576], P('row', 'col')
The draws below stay inside these ranges and needn't reach their ends.
All inputs are finite; a program needn't handle non-finite values.
Results may differ from the reference program's by a relative error of at most 0.014.
Values may be sent and summed in bfloat16 or wider, within the bound.
A program may use at most 128 MiB of HBM per device.

```python
import jax
import jax.numpy as jnp
from jax import lax

D = 6144
FF = 24576
TOKENS = 512
N_COL = 8


def with_spikes(values, stream_key, source, target, parts, factor):
    def block_of(position):
        return (jnp.arange(values.shape[position]) // (values.shape[position] // parts)).reshape((-1,) + (1,) * (values.ndim - 1 - position))

    first = jax.random.permutation(stream_key, parts)[block_of(target)]
    far = (block_of(target) + parts // 2) % parts
    return jnp.where((block_of(source) == first) | (block_of(source) == far), factor * values, values)


def block_scale(key, extent, split, least, high):
    level, own = 1.0, jax.random.fold_in(key, 6)
    for position, parts in split:
        draws = jnp.exp(jax.random.uniform(jax.random.fold_in(own, position), (parts,), jnp.float32, least / len(split), high / len(split)))
        level = level * jnp.repeat(draws, extent[position] // parts).reshape([-1 if axis == position else 1 for axis in range(len(extent))])
    return level


def scatter_about(stream_key, extent, width, bound, split=(), kind=jnp.bfloat16):
    factor_of = block_scale(stream_key, extent, split, -0.22, 0.18) if split else 1.0
    drawn = jax.random.normal(stream_key, extent, jnp.float32) * width * factor_of
    return jnp.minimum(jnp.maximum(drawn, -bound), bound).astype(kind)


def bell_draw_with(key, shape, width, most, cuts, heavy, held_as=jnp.bfloat16):
    array = width * jax.random.normal(key, shape, jnp.float32)
    if cuts:
        array = array * block_scale(key, shape, cuts, -0.22, 0.18)
    return jnp.clip(with_spikes(array, jax.random.fold_in(key, 3), *heavy), -most, most).astype(held_as)


def setup_inputs(seed: int = 0) -> dict:
    key_list = jax.random.split(jax.random.key(seed), 4)
    tokens = scatter_about(key_list[0], (TOKENS, D), 1.0, 6.0, ((0, 4), (1, 8)))
    weight = scatter_about(key_list[1], (D, FF), D ** -0.5, 0.078125, ((0, 4), (1, 8)))
    act_grad = bell_draw_with(key_list[2], (TOKENS, FF), 1.0, 6.0, ((0, 4), (1, 8)), (1, 0, 8, 2.0))
    return dict(tokens=tokens, weight=weight, act_grad=act_grad)


root_two_pi = 0.7978845608028654
cubic_coef = 0.044715


def gelu_tanh(value):
    return 0.5 * value * (1.0 + jnp.tanh(root_two_pi * (value + cubic_coef * value * value * value)))


def gelu_slope(value):
    angle = jnp.tanh(root_two_pi * (value + cubic_coef * value * value * value))
    return 0.5 * (1.0 + angle) + 0.5 * value * (1.0 - angle * angle) * root_two_pi * (1.0 + 3.0 * cubic_coef * value * value)


def reference(tokens, weight, act_grad):
    hidden_pre = jnp.dot(tokens, weight, preferred_element_type=jnp.float32)
    activation = gelu_tanh(hidden_pre).astype(jnp.bfloat16)
    hidden_grad = (act_grad.astype(jnp.float32) * gelu_slope(hidden_pre)).astype(jnp.bfloat16)
    weight_grad = jnp.dot(tokens.T, hidden_grad, preferred_element_type=jnp.float32).astype(jnp.bfloat16)
    block_width = FF // N_COL

    def step(running, block_index):
        offset = (block_index * block_width).astype(jnp.int32)
        hidden_block = lax.dynamic_slice_in_dim(hidden_grad, offset, block_width, 1)
        weight_block = lax.dynamic_slice_in_dim(weight, offset, block_width, 1)
        partial_value = jnp.dot(hidden_block, weight_block.T, preferred_element_type=jnp.float32)
        partial_value = lax.optimization_barrier(partial_value.astype(jnp.bfloat16)).astype(jnp.float32)
        return running + partial_value, None

    initial = jnp.zeros((TOKENS, D), jnp.float32)
    summed, unused = lax.scan(step, initial, jnp.arange(N_COL, dtype=jnp.int32))
    input_grad = summed.astype(jnp.bfloat16)
    return activation, input_grad, weight_grad
```

```python
import jax
import jax.numpy as jnp
from jax import lax
from jax.sharding import PartitionSpec as P

root_two_pi = 0.7978845608028654
cubic_coef = 0.044715


def gelu_tanh(value):
    return (
        0.5 * value * (1.0 + jnp.tanh(root_two_pi * (value + cubic_coef * value * value * value)))
    )


def gelu_slope(value):
    angle = jnp.tanh(root_two_pi * (value + cubic_coef * value * value * value))
    return 0.5 * (1.0 + angle) + 0.5 * value * (1.0 - angle * angle) * root_two_pi * (
        1.0 + 3.0 * cubic_coef * value * value
    )


def local(tokens, weight, act_grad):
    row_block = lax.all_gather(tokens, "col", axis=1, tiled=True)
    token_cols = lax.all_to_all(row_block, "row", split_axis=1, concat_axis=0, tiled=True)
    partial_pre = jnp.dot(token_cols, weight, preferred_element_type=jnp.float32)
    hidden_pre = lax.psum_scatter(
        partial_pre.astype(jnp.bfloat16), "row", scatter_dimension=0, tiled=True
    ).astype(jnp.float32)
    activation = gelu_tanh(hidden_pre).astype(jnp.bfloat16)
    hidden_grad = (act_grad.astype(jnp.float32) * gelu_slope(hidden_pre)).astype(jnp.bfloat16)
    all_hidden = lax.all_gather(hidden_grad, "row", axis=0, tiled=True)
    weight_grad = lax.dot_general(
        token_cols, all_hidden, (((0,), (0,)), ((), ())), preferred_element_type=jnp.float32
    ).astype(jnp.bfloat16)
    input_grad = lax.psum_scatter(
        lax.dot_general(
            all_hidden, weight, (((1,), (1,)), ((), ())), preferred_element_type=jnp.float32
        ).astype(jnp.bfloat16),
        "col",
        scatter_dimension=0,
        tiled=True,
    )
    return (activation, input_grad, weight_grad)


def solution(mesh):
    placed = (P("row", "col"), P("row", "col"), P("row", "col"))
    return jax.shard_map(
        local,
        mesh=mesh,
        in_specs=placed,
        out_specs=(P("row", "col"), P("col", "row"), P("row", "col")),
        check_vma=False,
    )
```

```python
import functools

import jax
import jax.numpy as jnp
from jax import lax
from jax.experimental import pallas as pl
from jax.experimental.pallas import tpu as pltpu
from jax.sharding import PartitionSpec as P

root_two_pi = 0.7978845608028654
cubic_coef = 0.044715
LAG = 1
WIDTH = 256


def grid_kernel(
    n, count, width, rows, lag,
    x_ref, xt_ref, w_hbm, g_ref,
    act_ref, dx_ref, dw_hbm,
    w_v, p_v, stage, from_low, from_high, hidden, dx_acc, dw_v,
    w_sem, dw_sem, low_sem, high_sem, ag_sem, rs_send, up_send, down_send,
):
    z = lax.axis_index("row")
    bf16, f32 = jnp.bfloat16, jnp.float32

    def w_copy(k):
        cols = pl.ds(pl.multiple_of(k * width, width), width)
        return pltpu.make_async_copy(w_hbm.at[:, cols], w_v.at[k], w_sem.at[k])

    def dw_copy(k):
        cols = pl.ds(pl.multiple_of(k * width, width), width)
        return pltpu.make_async_copy(dw_v.at[lax.rem(k, 2)], dw_hbm.at[:, cols], dw_sem.at[lax.rem(k, 2)])

    def block(t):
        return pl.ds(t * rows, rows)

    def send_up(src, dst, send, recv):
        return pltpu.make_async_remote_copy(src, dst, send, recv, device_id={"row": z + 1}, device_id_type=pl.DeviceIdType.MESH)

    def send_down(src, dst, send, recv):
        return pltpu.make_async_remote_copy(src, dst, send, recv, device_id={"row": z - 1}, device_id_type=pl.DeviceIdType.MESH)

    def rs_up(k, t):
        return send_up(stage.at[k, block(t)], from_low.at[k, block(t)], rs_send.at[k, t], low_sem.at[k, t])

    def rs_down(k, t):
        return send_down(stage.at[k, block(t)], from_high.at[k, block(t)], rs_send.at[k, t], high_sem.at[k, t])

    def ag_up(k, t):
        return send_up(hidden.at[k, block(t)], hidden.at[k, block(t)], up_send.at[k, t], ag_sem.at[k, t])

    def ag_down(k, t):
        return send_down(hidden.at[k, block(t)], hidden.at[k, block(t)], down_send.at[k, t], ag_sem.at[k, t])

    def inside(k):
        return jnp.logical_and(k >= 0, k < count)

    def both(a, b):
        return jnp.logical_and(a, b)

    def first_matmul(k):
        w_copy(k).wait()
        p_v[k] = jnp.dot(x_ref[...], w_v[k], preferred_element_type=f32)

    def start_w(k, carry):
        w_copy(k).start()
        return carry

    lax.fori_loop(0, count, start_w, 0)

    barrier = pltpu.get_barrier_semaphore()

    @pl.when(z > 0)
    def _():
        pl.semaphore_signal(barrier, inc=1, device_id={"row": z - 1}, device_id_type=pl.DeviceIdType.MESH)

    @pl.when(z < n - 1)
    def _():
        pl.semaphore_signal(barrier, inc=1, device_id={"row": z + 1}, device_id_type=pl.DeviceIdType.MESH)

    @pl.when(both(z > 0, z < n - 1))
    def _():
        pl.semaphore_wait(barrier, 2)

    @pl.when(jnp.logical_or(z == 0, z == n - 1))
    def _():
        pl.semaphore_wait(barrier, 1)

    dx_acc[...] = jnp.zeros_like(dx_acc)
    first_matmul(0)

    def step(s, carry):
        up_k = s - lag * z
        for t in range(n - 1, 0, -1):

            @pl.when(both(t > z, inside(up_k)))
            def _():
                @pl.when(z > 0)
                def _():
                    rs_up(up_k, t).wait_recv()
                    stage[up_k, block(t)] = (
                        p_v[up_k, block(t)] + from_low[up_k, block(t)].astype(f32)
                    ).astype(bf16)

                @pl.when(z == 0)
                def _():
                    stage[up_k, block(t)] = p_v[up_k, block(t)].astype(bf16)

                rs_up(up_k, t).start()

        down_k = s - lag * (n - 1 - z)
        for t in range(n - 1):

            @pl.when(both(t < z, inside(down_k)))
            def _():
                @pl.when(z < n - 1)
                def _():
                    rs_down(down_k, t).wait_recv()
                    stage[down_k, block(t)] = (
                        p_v[down_k, block(t)] + from_high[down_k, block(t)].astype(f32)
                    ).astype(bf16)

                @pl.when(z == n - 1)
                def _():
                    stage[down_k, block(t)] = p_v[down_k, block(t)].astype(bf16)

                rs_down(down_k, t).start()

        own_k = s - lag * (n - 1)

        @pl.when(inside(own_k))
        def _():
            mine = pl.ds(pl.multiple_of(z * rows, rows), rows)
            cols = pl.ds(pl.multiple_of(own_k * width, width), width)

            @pl.when(z > 0)
            def _():
                rs_up(own_k, z).wait_recv()
                p_v[own_k, mine] += from_low[own_k, mine].astype(f32)

            @pl.when(z < n - 1)
            def _():
                rs_down(own_k, z).wait_recv()
                p_v[own_k, mine] += from_high[own_k, mine].astype(f32)

            u = p_v[own_k, mine]
            angle = jnp.tanh(root_two_pi * (u + cubic_coef * u * u * u))
            act_ref[:, cols] = (0.5 * u * (1.0 + angle)).astype(bf16)
            slope = 0.5 * (1.0 + angle) + 0.5 * u * (1.0 - angle * angle) * root_two_pi * (
                1.0 + 3.0 * cubic_coef * u * u
            )
            hidden[own_k, mine] = (g_ref[:, cols].astype(f32) * slope).astype(bf16)

            @pl.when(z < n - 1)
            def _():
                ag_up(own_k, z).start()

            @pl.when(z > 0)
            def _():
                ag_down(own_k, z).start()

        for t in range(n):
            low_k = s - lag * (n - 1) - lag * (z - t)

            @pl.when(both(t < z, inside(low_k)))
            def _():
                ag_up(low_k, t).wait_recv()

                @pl.when(z < n - 1)
                def _():
                    ag_up(low_k, t).start()

            high_k = s - lag * (n - 1) - lag * (t - z)

            @pl.when(both(t > z, inside(high_k)))
            def _():
                ag_down(high_k, t).wait_recv()

                @pl.when(z > 0)
                def _():
                    ag_down(high_k, t).start()

        @pl.when(s + 1 < count)
        def _():
            first_matmul(s + 1)

        last_k = s - 2 * lag * (n - 1)

        @pl.when(inside(last_k))
        def _():
            @pl.when(last_k >= 2)
            def _():
                dw_copy(last_k - 2).wait()

            dw_v[lax.rem(last_k, 2)] = jnp.dot(
                xt_ref[...], hidden[last_k], preferred_element_type=f32
            ).astype(bf16)
            dw_copy(last_k).start()
            dx_acc[...] += lax.dot_general(
                hidden[last_k], w_v[last_k], (((1,), (1,)), ((), ())), preferred_element_type=f32
            )

        return carry

    lax.fori_loop(0, count + 2 * lag * (n - 1), step, 0)
    dx_ref[...] = dx_acc[...].astype(bf16)

    def finish(k, carry):
        for t in range(n):

            @pl.when(t > z)
            def _():
                rs_up(k, t).wait_send()

            @pl.when(t < z)
            def _():
                rs_down(k, t).wait_send()

            @pl.when(both(t <= z, z < n - 1))
            def _():
                ag_up(k, t).wait_send()

            @pl.when(both(t >= z, z > 0))
            def _():
                ag_down(k, t).wait_send()

        return carry

    lax.fori_loop(0, count, finish, 0)
    for k in range(max(0, count - 2), count):
        dw_copy(k).wait()


def pick_width(units):
    width = min(WIDTH, units)
    while units % width:
        width -= 128
    return width


def grid_call(n, x, weight, act_grad):
    tokens, depth = x.shape
    rows, units = act_grad.shape
    width = pick_width(units)
    count = units // width
    bf16, f32 = jnp.bfloat16, jnp.float32
    vmem = pl.BlockSpec(memory_space=pltpu.VMEM)
    hbm = pl.BlockSpec(memory_space=pl.ANY)
    chunks = (count, tokens, width)
    dma = pltpu.SemaphoreType.DMA
    return pl.pallas_call(
        functools.partial(grid_kernel, n, count, width, rows, LAG),
        out_shape=(
            jax.ShapeDtypeStruct((rows, units), bf16),
            jax.ShapeDtypeStruct((tokens, depth), bf16),
            jax.ShapeDtypeStruct((depth, units), bf16),
        ),
        in_specs=[vmem, vmem, hbm, vmem],
        out_specs=(vmem, vmem, hbm),
        scratch_shapes=[
            pltpu.VMEM((count, depth, width), bf16),
            pltpu.VMEM(chunks, f32),
            pltpu.VMEM(chunks, bf16),
            pltpu.VMEM(chunks, bf16),
            pltpu.VMEM(chunks, bf16),
            pltpu.VMEM(chunks, bf16),
            pltpu.VMEM((tokens, depth), f32),
            pltpu.VMEM((2, depth, width), bf16),
            dma((count,)),
            dma((2,)),
            dma((count, n)),
            dma((count, n)),
            dma((count, n)),
            dma((count, n)),
            dma((count, n)),
            dma((count, n)),
        ],
        compiler_params=pltpu.CompilerParams(
            collective_id=0, has_side_effects=True, vmem_limit_bytes=60 * 1024 * 1024
        ),
        cost_estimate=pl.CostEstimate(
            flops=6 * tokens * depth * units, bytes_accessed=4 * depth * units, transcendentals=rows * units
        ),
    )(x, x.T, weight, act_grad)


def local(n, tokens, weight, act_grad):
    row_block = lax.all_gather(tokens, "col", axis=1, tiled=True)
    token_cols = lax.all_to_all(row_block, "row", split_axis=1, concat_axis=0, tiled=True)
    activation, partial_grad, weight_grad = grid_call(n, token_cols, weight, act_grad)
    input_grad = lax.psum_scatter(partial_grad, "col", scatter_dimension=0, tiled=True)
    return (activation, input_grad, weight_grad)


def solution(mesh):
    placed = (P("row", "col"), P("row", "col"), P("row", "col"))
    return jax.shard_map(
        functools.partial(local, mesh.shape["row"]),
        mesh=mesh,
        in_specs=placed,
        out_specs=(P("row", "col"), P("col", "row"), P("row", "col")),
        check_vma=False,
    )
```

```python
import functools

import jax
import jax.numpy as jnp
from jax import lax
from jax.experimental import pallas as pl
from jax.experimental.pallas import tpu as pltpu
from jax.sharding import PartitionSpec as P

root_two_pi = 0.7978845608028654
cubic_coef = 0.044715
LAG = 1
WIDTH = 256
CHIPS = 4
CORES = 2


def grid_kernel(
    n, count, width, rows, lag, plane,
    x_in, w_hbm, g_ref,
    act_ref, dx_ref, dw_hbm,
    w_v, p_v, stage, from_low, from_high, hidden, dx_acc, dw_v, xt_ref,
    w_sem, dw_sem, low_sem, high_sem, ag_sem, rs_send, up_send, down_send,
    *extra,
):
    z = lax.axis_index("row")
    bf16, f32 = jnp.bfloat16, jnp.float32
    if plane:
        (
            x_ref, token_parts, z_parts, pair_out, pair_in, chip_out, chip_in,
            spread_send, spread_recv, z_send, z_recv, chip_send, chip_recv, pair_send, pair_recv,
            sum_pair_send, sum_pair_recv, sum_chip_send, sum_chip_recv,
        ) = extra
        col = lax.axis_index("col")
        chip, core = col // CORES, col % CORES
        half = x_in.shape[1]
        part = rows // CHIPS
    else:
        x_ref = x_in

    def w_copy(k):
        cols = pl.ds(pl.multiple_of(k * width, width), width)
        return pltpu.make_async_copy(w_hbm.at[:, cols], w_v.at[k], w_sem.at[k])

    def dw_copy(k):
        cols = pl.ds(pl.multiple_of(k * width, width), width)
        return pltpu.make_async_copy(dw_v.at[lax.rem(k, 2)], dw_hbm.at[:, cols], dw_sem.at[lax.rem(k, 2)])

    def block(t):
        return pl.ds(t * rows, rows)

    def send_up(src, dst, send, recv):
        return pltpu.make_async_remote_copy(src, dst, send, recv, device_id={"row": z + 1}, device_id_type=pl.DeviceIdType.MESH)

    def send_down(src, dst, send, recv):
        return pltpu.make_async_remote_copy(src, dst, send, recv, device_id={"row": z - 1}, device_id_type=pl.DeviceIdType.MESH)

    def rs_up(k, t):
        return send_up(stage.at[k, block(t)], from_low.at[k, block(t)], rs_send.at[k, t], low_sem.at[k, t])

    def rs_down(k, t):
        return send_down(stage.at[k, block(t)], from_high.at[k, block(t)], rs_send.at[k, t], high_sem.at[k, t])

    def ag_up(k, t):
        return send_up(hidden.at[k, block(t)], hidden.at[k, block(t)], up_send.at[k, t], ag_sem.at[k, t])

    def ag_down(k, t):
        return send_down(hidden.at[k, block(t)], hidden.at[k, block(t)], down_send.at[k, t], ag_sem.at[k, t])

    def inside(k):
        return jnp.logical_and(k >= 0, k < count)

    def both(a, b):
        return jnp.logical_and(a, b)

    def first_matmul(k):
        w_copy(k).wait()
        p_v[k] = jnp.dot(x_ref[...], w_v[k], preferred_element_type=f32)

    def start_w(k, carry):
        w_copy(k).start()
        return carry

    lax.fori_loop(0, count, start_w, 0)

    def line_barrier():
        barrier = pltpu.get_barrier_semaphore()

        @pl.when(z > 0)
        def _():
            pl.semaphore_signal(barrier, inc=1, device_id={"row": z - 1}, device_id_type=pl.DeviceIdType.MESH)

        @pl.when(z < n - 1)
        def _():
            pl.semaphore_signal(barrier, inc=1, device_id={"row": z + 1}, device_id_type=pl.DeviceIdType.MESH)

        @pl.when(both(z > 0, z < n - 1))
        def _():
            pl.semaphore_wait(barrier, 2)

        @pl.when(jnp.logical_or(z == 0, z == n - 1))
        def _():
            pl.semaphore_wait(barrier, 1)

    def to(row, column):
        return {"device_id": {"row": row, "col": column}, "device_id_type": pl.DeviceIdType.MESH}

    def other_chip(d):
        return ((chip + d) % CHIPS) * CORES + core

    def pair():
        return chip * CORES + 1 - core

    def spread(d):
        target = (chip + d) % CHIPS
        return pltpu.make_async_remote_copy(
            x_in.at[pl.ds(pl.multiple_of(target * part, part), part)], token_parts.at[chip],
            spread_send.at[d], spread_recv.at[d], **to(z, other_chip(d)),
        )

    def across(d):
        target = (z + d) % n
        return pltpu.make_async_remote_copy(
            token_parts.at[target], z_parts.at[z], z_send.at[d], z_recv.at[d], **to(target, col)
        )

    def place(origin, source_chip, source_core):
        return (
            pl.ds(pl.multiple_of(origin * rows + source_chip * part, part), part),
            pl.ds(pl.multiple_of(source_core * half, half), half),
        )

    def share(dz, d):
        origin = (z - dz + n) % n
        return pltpu.make_async_remote_copy(
            z_parts.at[origin], x_ref.at[place(origin, chip, core)],
            chip_send.at[dz, d], chip_recv.at[dz, d], **to(z, other_chip(d)),
        )

    def to_pair(dz, d):
        origin = (z - dz + n) % n
        where = place(origin, (chip - d + CHIPS) % CHIPS, core)
        return pltpu.make_async_remote_copy(
            x_ref.at[where], x_ref.at[where], pair_send.at[dz, d], pair_recv.at[dz, d], **to(z, pair())
        )

    def gather_tokens():
        for d in range(1, CHIPS):
            spread(d).start()
        token_parts[chip] = x_in[pl.ds(pl.multiple_of(chip * part, part), part), :]
        for d in range(1, CHIPS):
            spread(d).wait_recv()
        for d in range(1, n):
            across(d).start()
        z_parts[z] = token_parts[z]
        for dz in range(n):
            origin = (z - dz + n) % n
            if dz:
                across(dz).wait_recv()
            for d in (2, 1, 3):
                share(dz, d).start()
            x_ref[place(origin, chip, core)] = z_parts[origin]
            to_pair(dz, 0).start()
        for dz in range(n):
            for d in (1, 3, 2):
                share(dz, d).wait_recv()
                to_pair(dz, d).start()
        for dz in range(n):
            for d in range(CHIPS):
                to_pair(dz, d).wait_recv()

    def end_gather():
        for d in range(1, CHIPS):
            spread(d).wait_send()
        for d in range(1, n):
            across(d).wait_send()
        for dz in range(n):
            for d in range(CHIPS):
                to_pair(dz, d).wait_send()
                if d:
                    share(dz, d).wait_send()

    def sum_rows(d, which):
        size = dx_ref.shape[0]
        return pl.ds(pl.multiple_of((((chip + d) % CHIPS) * CORES + which) * size, size), size)

    def sum_pair(d):
        return pltpu.make_async_remote_copy(
            pair_out.at[d], pair_in.at[d], sum_pair_send.at[d], sum_pair_recv.at[d], **to(z, pair())
        )

    def sum_chip(d):
        return pltpu.make_async_remote_copy(
            chip_out.at[d], chip_in.at[d], sum_chip_send.at[d], sum_chip_recv.at[d], **to(z, other_chip(d))
        )

    def scatter_sum():
        order = (2, 1, 3, 0)
        for d in order:
            pair_out[d] = dx_acc[sum_rows(d, 1 - core), :].astype(bf16)
            sum_pair(d).start()
        for d in order:
            sum_pair(d).wait_recv()
            both_cores = dx_acc[sum_rows(d, core), :] + pair_in[d].astype(f32)
            if d:
                chip_out[d] = both_cores.astype(bf16)
                sum_chip(d).start()
            else:
                total = both_cores
        for d in range(1, CHIPS):
            sum_chip(d).wait_recv()
            total += chip_in[d].astype(f32)
        dx_ref[...] = total.astype(bf16)
        for d in order:
            sum_pair(d).wait_send()
            if d:
                sum_chip(d).wait_send()

    if plane:
        barrier = pltpu.get_barrier_semaphore()
        for d in range(1, n):
            pl.semaphore_signal(barrier, inc=1, **to((z + d) % n, col))
        for d in range(1, CHIPS):
            pl.semaphore_signal(barrier, inc=1, **to(z, other_chip(d)))
        pl.semaphore_signal(barrier, inc=1, **to(z, pair()))
        pl.semaphore_wait(barrier, n - 1 + CHIPS)
        gather_tokens()
    else:
        line_barrier()

    dx_acc[...] = jnp.zeros_like(dx_acc)
    first_matmul(0)

    def step(s, carry):
        up_k = s - lag * z
        for t in range(n - 1, 0, -1):

            @pl.when(both(t > z, inside(up_k)))
            def _():
                @pl.when(z > 0)
                def _():
                    rs_up(up_k, t).wait_recv()
                    stage[up_k, block(t)] = (
                        p_v[up_k, block(t)] + from_low[up_k, block(t)].astype(f32)
                    ).astype(bf16)

                @pl.when(z == 0)
                def _():
                    stage[up_k, block(t)] = p_v[up_k, block(t)].astype(bf16)

                rs_up(up_k, t).start()

        down_k = s - lag * (n - 1 - z)
        for t in range(n - 1):

            @pl.when(both(t < z, inside(down_k)))
            def _():
                @pl.when(z < n - 1)
                def _():
                    rs_down(down_k, t).wait_recv()
                    stage[down_k, block(t)] = (
                        p_v[down_k, block(t)] + from_high[down_k, block(t)].astype(f32)
                    ).astype(bf16)

                @pl.when(z == n - 1)
                def _():
                    stage[down_k, block(t)] = p_v[down_k, block(t)].astype(bf16)

                rs_down(down_k, t).start()

        own_k = s - lag * (n - 1)

        @pl.when(inside(own_k))
        def _():
            mine = pl.ds(pl.multiple_of(z * rows, rows), rows)
            cols = pl.ds(pl.multiple_of(own_k * width, width), width)

            @pl.when(z > 0)
            def _():
                rs_up(own_k, z).wait_recv()
                p_v[own_k, mine] += from_low[own_k, mine].astype(f32)

            @pl.when(z < n - 1)
            def _():
                rs_down(own_k, z).wait_recv()
                p_v[own_k, mine] += from_high[own_k, mine].astype(f32)

            u = p_v[own_k, mine]
            angle = jnp.tanh(root_two_pi * (u + cubic_coef * u * u * u))
            act_ref[:, cols] = (0.5 * u * (1.0 + angle)).astype(bf16)
            slope = 0.5 * (1.0 + angle) + 0.5 * u * (1.0 - angle * angle) * root_two_pi * (
                1.0 + 3.0 * cubic_coef * u * u
            )
            hidden[own_k, mine] = (g_ref[:, cols].astype(f32) * slope).astype(bf16)

            @pl.when(z < n - 1)
            def _():
                ag_up(own_k, z).start()

            @pl.when(z > 0)
            def _():
                ag_down(own_k, z).start()

        for t in range(n):
            low_k = s - lag * (n - 1) - lag * (z - t)

            @pl.when(both(t < z, inside(low_k)))
            def _():
                ag_up(low_k, t).wait_recv()

                @pl.when(z < n - 1)
                def _():
                    ag_up(low_k, t).start()

            high_k = s - lag * (n - 1) - lag * (t - z)

            @pl.when(both(t > z, inside(high_k)))
            def _():
                ag_down(high_k, t).wait_recv()

                @pl.when(z > 0)
                def _():
                    ag_down(high_k, t).start()

        @pl.when(s + 1 < count)
        def _():
            first_matmul(s + 1)

        @pl.when(s == 1)
        def _():
            xt_ref[...] = x_ref[...].T

        last_k = s - 2 * lag * (n - 1)

        @pl.when(inside(last_k))
        def _():
            @pl.when(last_k >= 2)
            def _():
                dw_copy(last_k - 2).wait()

            dw_v[lax.rem(last_k, 2)] = jnp.dot(
                xt_ref[...], hidden[last_k], preferred_element_type=f32
            ).astype(bf16)
            dw_copy(last_k).start()
            dx_acc[...] += lax.dot_general(
                hidden[last_k], w_v[last_k], (((1,), (1,)), ((), ())), preferred_element_type=f32
            )

        return carry

    lax.fori_loop(0, count + 2 * lag * (n - 1), step, 0)
    if plane:
        scatter_sum()
        end_gather()
    else:
        dx_ref[...] = dx_acc[...].astype(bf16)

    def finish(k, carry):
        for t in range(n):

            @pl.when(t > z)
            def _():
                rs_up(k, t).wait_send()

            @pl.when(t < z)
            def _():
                rs_down(k, t).wait_send()

            @pl.when(both(t <= z, z < n - 1))
            def _():
                ag_up(k, t).wait_send()

            @pl.when(both(t >= z, z > 0))
            def _():
                ag_down(k, t).wait_send()

        return carry

    lax.fori_loop(0, count, finish, 0)
    for k in range(max(0, count - 2), count):
        dw_copy(k).wait()


def pick_width(units):
    width = min(WIDTH, units)
    while units % width:
        width -= 128
    return width


def grid_call(n, plane, x, weight, act_grad):
    rows, units = act_grad.shape
    depth = weight.shape[0]
    tokens = n * rows
    width = pick_width(units)
    count = units // width
    bf16, f32 = jnp.bfloat16, jnp.float32
    vmem = pl.BlockSpec(memory_space=pltpu.VMEM)
    hbm = pl.BlockSpec(memory_space=pl.ANY)
    chunks = (count, tokens, width)
    dma = pltpu.SemaphoreType.DMA
    sum_rows = tokens // (CHIPS * CORES) if plane else tokens
    scratch = [
        pltpu.VMEM((count, depth, width), bf16),
        pltpu.VMEM(chunks, f32),
        pltpu.VMEM(chunks, bf16),
        pltpu.VMEM(chunks, bf16),
        pltpu.VMEM(chunks, bf16),
        pltpu.VMEM(chunks, bf16),
        pltpu.VMEM((tokens, depth), f32),
        pltpu.VMEM((2, depth, width), bf16),
        pltpu.VMEM((depth, tokens), bf16),
        dma((count,)),
        dma((2,)),
    ] + [dma((count, n))] * 6
    if plane:
        part = (rows // CHIPS, x.shape[1])
        scratch += [
            pltpu.VMEM((tokens, depth), bf16),
            pltpu.VMEM((CHIPS,) + part, bf16),
            pltpu.VMEM((n,) + part, bf16),
        ]
        scratch += [pltpu.VMEM((CHIPS, sum_rows, depth), bf16)] * 4
        scratch += [dma((CHIPS,))] * 2 + [dma((n,))] * 2 + [dma((n, CHIPS))] * 4 + [dma((CHIPS,))] * 4
    return pl.pallas_call(
        functools.partial(grid_kernel, n, count, width, rows, LAG, plane),
        out_shape=(
            jax.ShapeDtypeStruct((rows, units), bf16),
            jax.ShapeDtypeStruct((sum_rows, depth), bf16),
            jax.ShapeDtypeStruct((depth, units), bf16),
        ),
        in_specs=[vmem, hbm, vmem],
        out_specs=(vmem, vmem, hbm),
        scratch_shapes=scratch,
        compiler_params=pltpu.CompilerParams(
            collective_id=0, has_side_effects=True, vmem_limit_bytes=60 * 1024 * 1024
        ),
        cost_estimate=pl.CostEstimate(
            flops=6 * tokens * depth * units, bytes_accessed=4 * depth * units, transcendentals=rows * units
        ),
    )(x, weight, act_grad)


def local(n, columns, tokens, weight, act_grad):
    rows, part = tokens.shape
    if n == CHIPS and columns == CHIPS * CORES and rows % (16 * CHIPS) == 0 and part % 128 == 0:
        return grid_call(n, True, tokens, weight, act_grad)
    row_block = lax.all_gather(tokens, "col", axis=1, tiled=True)
    token_cols = lax.all_to_all(row_block, "row", split_axis=1, concat_axis=0, tiled=True)
    activation, partial_grad, weight_grad = grid_call(n, False, token_cols, weight, act_grad)
    input_grad = lax.psum_scatter(partial_grad, "col", scatter_dimension=0, tiled=True)
    return (activation, input_grad, weight_grad)


def solution(mesh):
    placed = (P("row", "col"), P("row", "col"), P("row", "col"))
    return jax.shard_map(
        functools.partial(local, mesh.shape["row"], mesh.shape["col"]),
        mesh=mesh,
        in_specs=placed,
        out_specs=(P("row", "col"), P("col", "row"), P("row", "col")),
        check_vma=False,
    )
```

```python
import functools

import jax
import jax.numpy as jnp
from jax import lax
from jax.experimental import pallas as pl
from jax.experimental.pallas import tpu as pltpu
from jax.sharding import PartitionSpec as P

root_two_pi = 0.7978845608028654
cubic_coef = 0.044715
LAG = 1
WIDTH = 256
CHIPS = 4
CORES = 2


def grid_kernel(
    n, count, width, rows, lag, plane,
    x_in, w_hbm, g_hbm,
    act_ref, dx_ref, dw_hbm,
    w_v, p_v, stage, from_low, from_high, hidden, dx_acc, dw_v, xt_ref,
    g_ref, g_sem, w_sem, dw_sem, low_sem, high_sem, ag_sem, rs_send, up_send, down_send,
    *extra,
):
    z = lax.axis_index("row")
    bf16, f32 = jnp.bfloat16, jnp.float32
    if plane:
        (
            x_ref, token_parts, z_parts, pair_out, pair_in, chip_out, chip_in,
            spread_send, spread_recv, z_send, z_recv, chip_send, chip_recv, pair_send, pair_recv,
            sum_pair_send, sum_pair_recv, sum_chip_send, sum_chip_recv,
        ) = extra
        col = lax.axis_index("col")
        chip, core = col // CORES, col % CORES
        half = x_in.shape[1]
        part = rows // CHIPS
    else:
        x_ref = x_in

    def w_copy(k):
        cols = pl.ds(pl.multiple_of(k * width, width), width)
        return pltpu.make_async_copy(w_hbm.at[:, cols], w_v.at[k], w_sem.at[k])

    def dw_copy(k):
        cols = pl.ds(pl.multiple_of(k * width, width), width)
        return pltpu.make_async_copy(dw_v.at[lax.rem(k, 2)], dw_hbm.at[:, cols], dw_sem.at[lax.rem(k, 2)])

    def block(t):
        return pl.ds(t * rows, rows)

    def send_up(src, dst, send, recv):
        return pltpu.make_async_remote_copy(src, dst, send, recv, device_id={"row": z + 1}, device_id_type=pl.DeviceIdType.MESH)

    def send_down(src, dst, send, recv):
        return pltpu.make_async_remote_copy(src, dst, send, recv, device_id={"row": z - 1}, device_id_type=pl.DeviceIdType.MESH)

    def rs_up(k, t):
        return send_up(stage.at[k, block(t)], from_low.at[k, block(t)], rs_send.at[k, t], low_sem.at[k, t])

    def rs_down(k, t):
        return send_down(stage.at[k, block(t)], from_high.at[k, block(t)], rs_send.at[k, t], high_sem.at[k, t])

    def ag_up(k, t):
        return send_up(hidden.at[k, block(t)], hidden.at[k, block(t)], up_send.at[k, t], ag_sem.at[k, t])

    def ag_down(k, t):
        return send_down(hidden.at[k, block(t)], hidden.at[k, block(t)], down_send.at[k, t], ag_sem.at[k, t])

    def inside(k):
        return jnp.logical_and(k >= 0, k < count)

    def both(a, b):
        return jnp.logical_and(a, b)

    def first_matmul(k):
        w_copy(k).wait()
        p_v[k] = jnp.dot(x_ref[...], w_v[k], preferred_element_type=f32)

    def start_w(k, carry):
        w_copy(k).start()
        return carry

    g_copy = pltpu.make_async_copy(g_hbm, g_ref, g_sem)
    g_copy.start()
    lax.fori_loop(0, count, start_w, 0)

    def line_barrier():
        barrier = pltpu.get_barrier_semaphore()

        @pl.when(z > 0)
        def _():
            pl.semaphore_signal(barrier, inc=1, device_id={"row": z - 1}, device_id_type=pl.DeviceIdType.MESH)

        @pl.when(z < n - 1)
        def _():
            pl.semaphore_signal(barrier, inc=1, device_id={"row": z + 1}, device_id_type=pl.DeviceIdType.MESH)

        @pl.when(both(z > 0, z < n - 1))
        def _():
            pl.semaphore_wait(barrier, 2)

        @pl.when(jnp.logical_or(z == 0, z == n - 1))
        def _():
            pl.semaphore_wait(barrier, 1)

    def to(row, column):
        return {"device_id": {"row": row, "col": column}, "device_id_type": pl.DeviceIdType.MESH}

    def other_chip(d):
        return ((chip + d) % CHIPS) * CORES + core

    def pair():
        return chip * CORES + 1 - core

    def spread(d):
        target = (chip + d) % CHIPS
        return pltpu.make_async_remote_copy(
            x_in.at[pl.ds(pl.multiple_of(target * part, part), part)], token_parts.at[chip],
            spread_send.at[d], spread_recv.at[d], **to(z, other_chip(d)),
        )

    def across(d):
        target = (z + d) % n
        return pltpu.make_async_remote_copy(
            token_parts.at[target], z_parts.at[z], z_send.at[d], z_recv.at[d], **to(target, col)
        )

    def place(origin, source_chip, source_core):
        return (
            pl.ds(pl.multiple_of(origin * rows + source_chip * part, part), part),
            pl.ds(pl.multiple_of(source_core * half, half), half),
        )

    def share(dz, d):
        origin = (z - dz + n) % n
        return pltpu.make_async_remote_copy(
            z_parts.at[origin], x_ref.at[place(origin, chip, core)],
            chip_send.at[dz, d], chip_recv.at[dz, d], **to(z, other_chip(d)),
        )

    def to_pair(dz, d):
        origin = (z - dz + n) % n
        where = place(origin, (chip - d + CHIPS) % CHIPS, core)
        return pltpu.make_async_remote_copy(
            x_ref.at[where], x_ref.at[where], pair_send.at[dz, d], pair_recv.at[dz, d], **to(z, pair())
        )

    def gather_tokens():
        for d in range(1, CHIPS):
            spread(d).start()
        token_parts[chip] = x_in[pl.ds(pl.multiple_of(chip * part, part), part), :]
        for d in range(1, CHIPS):
            spread(d).wait_recv()
        for d in range(1, n):
            across(d).start()
        z_parts[z] = token_parts[z]
        for dz in range(n):
            origin = (z - dz + n) % n
            if dz:
                across(dz).wait_recv()
            for d in (2, 1, 3):
                share(dz, d).start()
            x_ref[place(origin, chip, core)] = z_parts[origin]
            to_pair(dz, 0).start()
        for dz in range(n):
            for d in (1, 3, 2):
                share(dz, d).wait_recv()
                to_pair(dz, d).start()
        for dz in range(n):
            for d in range(CHIPS):
                to_pair(dz, d).wait_recv()

    def end_gather():
        for d in range(1, CHIPS):
            spread(d).wait_send()
        for d in range(1, n):
            across(d).wait_send()
        for dz in range(n):
            for d in range(CHIPS):
                to_pair(dz, d).wait_send()
                if d:
                    share(dz, d).wait_send()

    def sum_rows(t, which):
        size = dx_ref.shape[0]
        return pl.ds(pl.multiple_of((t * CORES + which) * size, size), size)

    def sum_pair(t):
        return pltpu.make_async_remote_copy(
            pair_out.at[t], pair_in.at[t], sum_pair_send.at[t], sum_pair_recv.at[t], **to(z, pair())
        )

    def sum_chip(t):
        return pltpu.make_async_remote_copy(
            chip_out.at[t], chip_in.at[chip], sum_chip_send.at[t], sum_chip_recv.at[chip], **to(z, t * CORES + core)
        )

    def sum_from(t):
        return pltpu.make_async_remote_copy(
            chip_out.at[t], chip_in.at[t], sum_chip_send.at[t], sum_chip_recv.at[t], **to(z, t * CORES + core)
        )

    def give_pair(t):
        pair_out[t] = dx_acc[sum_rows(t, 1 - core), :].astype(bf16)
        sum_pair(t).start()

    def give_chip(t):
        sum_pair(t).wait_recv()
        both_cores = dx_acc[sum_rows(t, core), :] + pair_in[t].astype(f32)

        @pl.when(chip != t)
        def _():
            chip_out[t] = both_cores.astype(bf16)
            sum_chip(t).start()

        @pl.when(chip == t)
        def _():
            dx_acc[sum_rows(t, core), :] = both_cores

    def end_sum():
        mine = sum_rows(chip, core)
        for t in range(CHIPS):

            @pl.when(chip != t)
            def _():
                sum_from(t).wait_recv()
                dx_acc[mine, :] += chip_in[t].astype(f32)

        dx_ref[...] = dx_acc[mine, :].astype(bf16)
        for t in range(CHIPS):
            sum_pair(t).wait_send()

            @pl.when(chip != t)
            def _():
                sum_chip(t).wait_send()

    if plane:
        barrier = pltpu.get_barrier_semaphore()
        for d in range(1, n):
            pl.semaphore_signal(barrier, inc=1, **to((z + d) % n, col))
        for d in range(1, CHIPS):
            pl.semaphore_signal(barrier, inc=1, **to(z, other_chip(d)))
        pl.semaphore_signal(barrier, inc=1, **to(z, pair()))
        pl.semaphore_wait(barrier, n - 1 + CHIPS)
        gather_tokens()
    else:
        line_barrier()

    dx_acc[...] = jnp.zeros_like(dx_acc)
    first_matmul(0)
    g_copy.wait()

    def step(s, carry):
        up_k = s - lag * z
        for t in range(n - 1, 0, -1):

            @pl.when(both(t > z, inside(up_k)))
            def _():
                @pl.when(z > 0)
                def _():
                    rs_up(up_k, t).wait_recv()
                    stage[up_k, block(t)] = (
                        p_v[up_k, block(t)] + from_low[up_k, block(t)].astype(f32)
                    ).astype(bf16)

                @pl.when(z == 0)
                def _():
                    stage[up_k, block(t)] = p_v[up_k, block(t)].astype(bf16)

                rs_up(up_k, t).start()

        down_k = s - lag * (n - 1 - z)
        for t in range(n - 1):

            @pl.when(both(t < z, inside(down_k)))
            def _():
                @pl.when(z < n - 1)
                def _():
                    rs_down(down_k, t).wait_recv()
                    stage[down_k, block(t)] = (
                        p_v[down_k, block(t)] + from_high[down_k, block(t)].astype(f32)
                    ).astype(bf16)

                @pl.when(z == n - 1)
                def _():
                    stage[down_k, block(t)] = p_v[down_k, block(t)].astype(bf16)

                rs_down(down_k, t).start()

        own_k = s - lag * jnp.maximum(z, n - 1 - z)

        @pl.when(inside(own_k))
        def _():
            mine = pl.ds(pl.multiple_of(z * rows, rows), rows)
            cols = pl.ds(pl.multiple_of(own_k * width, width), width)

            @pl.when(z > 0)
            def _():
                rs_up(own_k, z).wait_recv()
                p_v[own_k, mine] += from_low[own_k, mine].astype(f32)

            @pl.when(z < n - 1)
            def _():
                rs_down(own_k, z).wait_recv()
                p_v[own_k, mine] += from_high[own_k, mine].astype(f32)

            u = p_v[own_k, mine]
            angle = jnp.tanh(root_two_pi * (u + cubic_coef * u * u * u))
            act_ref[:, cols] = (0.5 * u * (1.0 + angle)).astype(bf16)
            slope = 0.5 * (1.0 + angle) + 0.5 * u * (1.0 - angle * angle) * root_two_pi * (
                1.0 + 3.0 * cubic_coef * u * u
            )
            hidden[own_k, mine] = (g_ref[:, cols].astype(f32) * slope).astype(bf16)

            @pl.when(z < n - 1)
            def _():
                ag_up(own_k, z).start()

            @pl.when(z > 0)
            def _():
                ag_down(own_k, z).start()

        for t in range(n):
            low_k = s - lag * max(t, n - 1 - t) - lag * (z - t)

            @pl.when(both(t < z, inside(low_k)))
            def _():
                ag_up(low_k, t).wait_recv()

                @pl.when(z < n - 1)
                def _():
                    ag_up(low_k, t).start()

            high_k = s - lag * max(t, n - 1 - t) - lag * (t - z)

            @pl.when(both(t > z, inside(high_k)))
            def _():
                ag_down(high_k, t).wait_recv()

                @pl.when(z > 0)
                def _():
                    ag_down(high_k, t).start()

        for t in range(n):
            sum_k = s - lag * (max(t, n - 1 - t) + jnp.maximum(z - t, t - z))

            @pl.when(inside(sum_k))
            def _():
                dx_acc[block(t), :] += lax.dot_general(
                    hidden[sum_k, block(t)], w_v[sum_k], (((1,), (1,)), ((), ())), preferred_element_type=f32
                )

            if plane:

                @pl.when(sum_k == count - 1)
                def _():
                    give_pair(t)

                @pl.when(sum_k == count)
                def _():
                    give_chip(t)

        @pl.when(s + 1 < count)
        def _():
            first_matmul(s + 1)

        @pl.when(s == 1)
        def _():
            xt_ref[...] = x_ref[...].T

        last_k = s - 2 * lag * (n - 1)

        @pl.when(inside(last_k))
        def _():
            @pl.when(last_k >= 2)
            def _():
                dw_copy(last_k - 2).wait()

            dw_v[lax.rem(last_k, 2)] = jnp.dot(
                xt_ref[...], hidden[last_k], preferred_element_type=f32
            ).astype(bf16)
            dw_copy(last_k).start()

        return carry

    lax.fori_loop(0, count + 2 * lag * (n - 1) + 1, step, 0)
    if plane:
        end_sum()
        end_gather()
    else:
        dx_ref[...] = dx_acc[...].astype(bf16)

    def finish(k, carry):
        for t in range(n):

            @pl.when(t > z)
            def _():
                rs_up(k, t).wait_send()

            @pl.when(t < z)
            def _():
                rs_down(k, t).wait_send()

            @pl.when(both(t <= z, z < n - 1))
            def _():
                ag_up(k, t).wait_send()

            @pl.when(both(t >= z, z > 0))
            def _():
                ag_down(k, t).wait_send()

        return carry

    lax.fori_loop(0, count, finish, 0)
    for k in range(max(0, count - 2), count):
        dw_copy(k).wait()


def pick_width(units):
    width = min(WIDTH, units)
    while units % width:
        width -= 128
    return width


def grid_call(n, plane, x, weight, act_grad):
    rows, units = act_grad.shape
    depth = weight.shape[0]
    tokens = n * rows
    width = pick_width(units)
    count = units // width
    bf16, f32 = jnp.bfloat16, jnp.float32
    vmem = pl.BlockSpec(memory_space=pltpu.VMEM)
    hbm = pl.BlockSpec(memory_space=pl.ANY)
    chunks = (count, tokens, width)
    dma = pltpu.SemaphoreType.DMA
    sum_rows = tokens // (CHIPS * CORES) if plane else tokens
    scratch = [
        pltpu.VMEM((count, depth, width), bf16),
        pltpu.VMEM(chunks, f32),
        pltpu.VMEM(chunks, bf16),
        pltpu.VMEM(chunks, bf16),
        pltpu.VMEM(chunks, bf16),
        pltpu.VMEM(chunks, bf16),
        pltpu.VMEM((tokens, depth), f32),
        pltpu.VMEM((2, depth, width), bf16),
        pltpu.VMEM((depth, tokens), bf16),
        pltpu.VMEM((rows, units), bf16),
        dma,
        dma((count,)),
        dma((2,)),
    ] + [dma((count, n))] * 6
    if plane:
        part = (rows // CHIPS, x.shape[1])
        scratch += [
            pltpu.VMEM((tokens, depth), bf16),
            pltpu.VMEM((CHIPS,) + part, bf16),
            pltpu.VMEM((n,) + part, bf16),
        ]
        scratch += [pltpu.VMEM((CHIPS, sum_rows, depth), bf16)] * 4
        scratch += [dma((CHIPS,))] * 2 + [dma((n,))] * 2 + [dma((n, CHIPS))] * 4 + [dma((CHIPS,))] * 4
    return pl.pallas_call(
        functools.partial(grid_kernel, n, count, width, rows, LAG, plane),
        out_shape=(
            jax.ShapeDtypeStruct((rows, units), bf16),
            jax.ShapeDtypeStruct((sum_rows, depth), bf16),
            jax.ShapeDtypeStruct((depth, units), bf16),
        ),
        in_specs=[vmem, hbm, hbm],
        out_specs=(vmem, vmem, hbm),
        scratch_shapes=scratch,
        compiler_params=pltpu.CompilerParams(
            collective_id=0, has_side_effects=True, vmem_limit_bytes=60 * 1024 * 1024
        ),
        cost_estimate=pl.CostEstimate(
            flops=6 * tokens * depth * units, bytes_accessed=4 * depth * units, transcendentals=rows * units
        ),
    )(x, weight, act_grad)


def local(n, columns, tokens, weight, act_grad):
    rows, part = tokens.shape
    if n == CHIPS and columns == CHIPS * CORES and rows % (16 * CHIPS) == 0 and part % 128 == 0:
        return grid_call(n, True, tokens, weight, act_grad)
    row_block = lax.all_gather(tokens, "col", axis=1, tiled=True)
    token_cols = lax.all_to_all(row_block, "row", split_axis=1, concat_axis=0, tiled=True)
    activation, partial_grad, weight_grad = grid_call(n, False, token_cols, weight, act_grad)
    input_grad = lax.psum_scatter(partial_grad, "col", scatter_dimension=0, tiled=True)
    return (activation, input_grad, weight_grad)


def solution(mesh):
    placed = (P("row", "col"), P("row", "col"), P("row", "col"))
    return jax.shard_map(
        functools.partial(local, mesh.shape["row"], mesh.shape["col"]),
        mesh=mesh,
        in_specs=placed,
        out_specs=(P("row", "col"), P("col", "row"), P("row", "col")),
        check_vma=False,
    )
```

```python
import functools

import jax
import jax.numpy as jnp
from jax import lax
from jax.experimental import pallas as pl
from jax.experimental.pallas import tpu as pltpu
from jax.sharding import PartitionSpec as P

root_two_pi = 0.7978845608028654
cubic_coef = 0.044715
LAG = 1
WIDTH = 256
CHIPS = 4
CORES = 2


def grid_kernel(
    n, count, width, rows, lag, plane,
    x_in, w_hbm, g_hbm,
    act_ref, dx_ref, dw_hbm,
    w_v, p_v, stage, from_low, from_high, hidden, dx_acc, dw_v, xt_ref,
    g_ref, g_sem, w_sem, dw_sem, low_sem, high_sem, ag_sem, rs_send, up_send, down_send,
    *extra,
):
    z = lax.axis_index("row")
    bf16, f32 = jnp.bfloat16, jnp.float32
    if plane:
        (
            x_ref, token_parts, z_parts, pair_out, pair_in, chip_out, chip_in,
            spread_send, spread_recv, z_send, z_recv, chip_send, chip_recv, pair_send, pair_recv,
            sum_pair_send, sum_pair_recv, sum_chip_send, sum_chip_recv,
        ) = extra
        col = lax.axis_index("col")
        chip, core = col // CORES, col % CORES
        half = x_in.shape[1]
        part = rows // CHIPS
    else:
        x_ref = x_in

    def w_copy(k):
        cols = pl.ds(pl.multiple_of(k * width, width), width)
        return pltpu.make_async_copy(w_hbm.at[:, cols], w_v.at[k], w_sem.at[k])

    def dw_copy(k):
        cols = pl.ds(pl.multiple_of(k * width, width), width)
        return pltpu.make_async_copy(dw_v.at[lax.rem(k, 2)], dw_hbm.at[:, cols], dw_sem.at[lax.rem(k, 2)])

    def block(t):
        return pl.ds(t * rows if isinstance(t, int) else pl.multiple_of(t * rows, rows), rows)

    def send_up(src, dst, send, recv):
        return pltpu.make_async_remote_copy(src, dst, send, recv, device_id={"row": z + 1}, device_id_type=pl.DeviceIdType.MESH)

    def send_down(src, dst, send, recv):
        return pltpu.make_async_remote_copy(src, dst, send, recv, device_id={"row": z - 1}, device_id_type=pl.DeviceIdType.MESH)

    def rs_up(k, t):
        return send_up(stage.at[k, block(t)], from_low.at[k, block(t)], rs_send.at[k, t], low_sem.at[k, t])

    def rs_down(k, t):
        return send_down(stage.at[k, block(t)], from_high.at[k, block(t)], rs_send.at[k, t], high_sem.at[k, t])

    def ag_up(k, t):
        return send_up(hidden.at[k, block(t)], hidden.at[k, block(t)], up_send.at[k, t], ag_sem.at[k, t])

    def ag_down(k, t):
        return send_down(hidden.at[k, block(t)], hidden.at[k, block(t)], down_send.at[k, t], ag_sem.at[k, t])

    def inside(k):
        return jnp.logical_and(k >= 0, k < count)

    def both(a, b):
        return jnp.logical_and(a, b)

    def first_matmul(k):
        w_copy(k).wait()
        p_v[k] = jnp.dot(x_ref[...], w_v[k], preferred_element_type=f32)

    def start_w(k, carry):
        w_copy(k).start()
        return carry

    g_copy = pltpu.make_async_copy(g_hbm, g_ref, g_sem)
    g_copy.start()
    lax.fori_loop(0, count, start_w, 0)

    def line_barrier():
        barrier = pltpu.get_barrier_semaphore()

        @pl.when(z > 0)
        def _():
            pl.semaphore_signal(barrier, inc=1, device_id={"row": z - 1}, device_id_type=pl.DeviceIdType.MESH)

        @pl.when(z < n - 1)
        def _():
            pl.semaphore_signal(barrier, inc=1, device_id={"row": z + 1}, device_id_type=pl.DeviceIdType.MESH)

        @pl.when(both(z > 0, z < n - 1))
        def _():
            pl.semaphore_wait(barrier, 2)

        @pl.when(jnp.logical_or(z == 0, z == n - 1))
        def _():
            pl.semaphore_wait(barrier, 1)

    def to(row, column):
        return {"device_id": {"row": row, "col": column}, "device_id_type": pl.DeviceIdType.MESH}

    def other_chip(d):
        return ((chip + d) % CHIPS) * CORES + core

    def pair():
        return chip * CORES + 1 - core

    def spread(d):
        target = (chip + d) % CHIPS
        return pltpu.make_async_remote_copy(
            x_in.at[pl.ds(pl.multiple_of(target * part, part), part)], token_parts.at[chip],
            spread_send.at[d], spread_recv.at[d], **to(z, other_chip(d)),
        )

    def across(d):
        target = (z + d) % n
        return pltpu.make_async_remote_copy(
            token_parts.at[target], z_parts.at[z], z_send.at[d], z_recv.at[d], **to(target, col)
        )

    def place(origin, source_chip, source_core):
        return (
            pl.ds(pl.multiple_of(origin * rows + source_chip * part, part), part),
            pl.ds(pl.multiple_of(source_core * half, half), half),
        )

    def share(dz, d):
        origin = (z - dz + n) % n
        return pltpu.make_async_remote_copy(
            z_parts.at[origin], x_ref.at[place(origin, chip, core)],
            chip_send.at[dz, d], chip_recv.at[dz, d], **to(z, other_chip(d)),
        )

    def to_pair(dz, d):
        origin = (z - dz + n) % n
        where = place(origin, (chip - d + CHIPS) % CHIPS, core)
        return pltpu.make_async_remote_copy(
            x_ref.at[where], x_ref.at[where], pair_send.at[dz, d], pair_recv.at[dz, d], **to(z, pair())
        )

    def gather_tokens():
        for d in range(1, CHIPS):
            spread(d).start()
        token_parts[chip] = x_in[pl.ds(pl.multiple_of(chip * part, part), part), :]
        for d in range(1, CHIPS):
            spread(d).wait_recv()
        for d in range(1, n):
            across(d).start()
        z_parts[z] = token_parts[z]
        for dz in range(n):
            origin = (z - dz + n) % n
            if dz:
                across(dz).wait_recv()
            for d in (2, 1, 3):
                share(dz, d).start()
            x_ref[place(origin, chip, core)] = z_parts[origin]
            to_pair(dz, 0).start()
        for dz in range(n):
            for d in (1, 3, 2):
                share(dz, d).wait_recv()
                to_pair(dz, d).start()
            if dz:
                begin(dz - 1)
        begin(n - 1)

    def begin(dz):
        for d in range(CHIPS):
            to_pair(dz, d).wait_recv()
        if dz == 0:
            w_copy(0).wait()
        t = (z - dz + n) % n
        p_v[0, block(t)] = jnp.dot(x_ref[block(t), :], w_v[0], preferred_element_type=f32)
        if dz:

            @pl.when(z == 0)
            def _():
                stage[0, block(t)] = p_v[0, block(t)].astype(bf16)
                rs_up(0, t).start()

            @pl.when(z == n - 1)
            def _():
                stage[0, block(t)] = p_v[0, block(t)].astype(bf16)
                rs_down(0, t).start()

    def end_gather():
        for d in range(1, CHIPS):
            spread(d).wait_send()
        for d in range(1, n):
            across(d).wait_send()
        for dz in range(n):
            for d in range(CHIPS):
                to_pair(dz, d).wait_send()
                if d:
                    share(dz, d).wait_send()

    def sum_rows(t, which):
        size = dx_ref.shape[0]
        return pl.ds(pl.multiple_of((t * CORES + which) * size, size), size)

    def sum_pair(t):
        return pltpu.make_async_remote_copy(
            pair_out.at[t], pair_in.at[t], sum_pair_send.at[t], sum_pair_recv.at[t], **to(z, pair())
        )

    def sum_chip(t):
        return pltpu.make_async_remote_copy(
            chip_out.at[t], chip_in.at[chip], sum_chip_send.at[t], sum_chip_recv.at[chip], **to(z, t * CORES + core)
        )

    def sum_from(t):
        return pltpu.make_async_remote_copy(
            chip_out.at[t], chip_in.at[t], sum_chip_send.at[t], sum_chip_recv.at[t], **to(z, t * CORES + core)
        )

    def give_pair(t):
        pair_out[t] = dx_acc[sum_rows(t, 1 - core), :].astype(bf16)
        sum_pair(t).start()

    def give_chip(t):
        sum_pair(t).wait_recv()
        both_cores = dx_acc[sum_rows(t, core), :] + pair_in[t].astype(f32)

        @pl.when(chip != t)
        def _():
            chip_out[t] = both_cores.astype(bf16)
            sum_chip(t).start()

        @pl.when(chip == t)
        def _():
            dx_acc[sum_rows(t, core), :] = both_cores

    def end_sum():
        mine = sum_rows(chip, core)
        for t in range(CHIPS):

            @pl.when(chip != t)
            def _():
                sum_from(t).wait_recv()
                dx_acc[mine, :] += chip_in[t].astype(f32)

        dx_ref[...] = dx_acc[mine, :].astype(bf16)
        for t in range(CHIPS):
            sum_pair(t).wait_send()

            @pl.when(chip != t)
            def _():
                sum_chip(t).wait_send()

    if plane:
        barrier = pltpu.get_barrier_semaphore()
        for d in range(1, n):
            pl.semaphore_signal(barrier, inc=1, **to((z + d) % n, col))
        for d in range(1, CHIPS):
            pl.semaphore_signal(barrier, inc=1, **to(z, other_chip(d)))
        pl.semaphore_signal(barrier, inc=1, **to(z, pair()))
        pl.semaphore_wait(barrier, n - 1 + CHIPS)
        gather_tokens()
    else:
        line_barrier()

    dx_acc[...] = jnp.zeros_like(dx_acc)
    if not plane:
        first_matmul(0)
    g_copy.wait()

    begun = 1 if plane else 0

    def step(s, carry):
        up_k = s - lag * z
        for t in range(n - 1, 0, -1):

            @pl.when(both(both(t > z, inside(up_k)), jnp.logical_or(z > 0, up_k >= begun)))
            def _():
                @pl.when(z > 0)
                def _():
                    rs_up(up_k, t).wait_recv()
                    stage[up_k, block(t)] = (
                        p_v[up_k, block(t)] + from_low[up_k, block(t)].astype(f32)
                    ).astype(bf16)

                @pl.when(z == 0)
                def _():
                    stage[up_k, block(t)] = p_v[up_k, block(t)].astype(bf16)

                rs_up(up_k, t).start()

        down_k = s - lag * (n - 1 - z)
        for t in range(n - 1):

            @pl.when(both(both(t < z, inside(down_k)), jnp.logical_or(z < n - 1, down_k >= begun)))
            def _():
                @pl.when(z < n - 1)
                def _():
                    rs_down(down_k, t).wait_recv()
                    stage[down_k, block(t)] = (
                        p_v[down_k, block(t)] + from_high[down_k, block(t)].astype(f32)
                    ).astype(bf16)

                @pl.when(z == n - 1)
                def _():
                    stage[down_k, block(t)] = p_v[down_k, block(t)].astype(bf16)

                rs_down(down_k, t).start()

        own_k = s - lag * jnp.maximum(z, n - 1 - z)

        @pl.when(inside(own_k))
        def _():
            mine = pl.ds(pl.multiple_of(z * rows, rows), rows)
            cols = pl.ds(pl.multiple_of(own_k * width, width), width)

            @pl.when(z > 0)
            def _():
                rs_up(own_k, z).wait_recv()
                p_v[own_k, mine] += from_low[own_k, mine].astype(f32)

            @pl.when(z < n - 1)
            def _():
                rs_down(own_k, z).wait_recv()
                p_v[own_k, mine] += from_high[own_k, mine].astype(f32)

            u = p_v[own_k, mine]
            angle = jnp.tanh(root_two_pi * (u + cubic_coef * u * u * u))
            act_ref[:, cols] = (0.5 * u * (1.0 + angle)).astype(bf16)
            slope = 0.5 * (1.0 + angle) + 0.5 * u * (1.0 - angle * angle) * root_two_pi * (
                1.0 + 3.0 * cubic_coef * u * u
            )
            hidden[own_k, mine] = (g_ref[:, cols].astype(f32) * slope).astype(bf16)

            @pl.when(z < n - 1)
            def _():
                ag_up(own_k, z).start()

            @pl.when(z > 0)
            def _():
                ag_down(own_k, z).start()

        for t in range(n):
            low_k = s - lag * max(t, n - 1 - t) - lag * (z - t)

            @pl.when(both(t < z, inside(low_k)))
            def _():
                ag_up(low_k, t).wait_recv()

                @pl.when(z < n - 1)
                def _():
                    ag_up(low_k, t).start()

            high_k = s - lag * max(t, n - 1 - t) - lag * (t - z)

            @pl.when(both(t > z, inside(high_k)))
            def _():
                ag_down(high_k, t).wait_recv()

                @pl.when(z > 0)
                def _():
                    ag_down(high_k, t).start()

        for t in range(n):
            sum_k = s - lag * (max(t, n - 1 - t) + jnp.maximum(z - t, t - z))

            @pl.when(inside(sum_k))
            def _():
                dx_acc[block(t), :] += lax.dot_general(
                    hidden[sum_k, block(t)], w_v[sum_k], (((1,), (1,)), ((), ())), preferred_element_type=f32
                )

            if plane:

                @pl.when(sum_k == count - 1)
                def _():
                    give_pair(t)

                @pl.when(sum_k == count)
                def _():
                    give_chip(t)

        @pl.when(s + 1 < count)
        def _():
            first_matmul(s + 1)

        @pl.when(s == 1)
        def _():
            xt_ref[...] = x_ref[...].T

        last_k = s - 2 * lag * (n - 1)

        @pl.when(inside(last_k))
        def _():
            @pl.when(last_k >= 2)
            def _():
                dw_copy(last_k - 2).wait()

            dw_v[lax.rem(last_k, 2)] = jnp.dot(
                xt_ref[...], hidden[last_k], preferred_element_type=f32
            ).astype(bf16)
            dw_copy(last_k).start()

        return carry

    lax.fori_loop(0, count + 2 * lag * (n - 1) + 1, step, 0)
    if plane:
        end_sum()
        end_gather()
    else:
        dx_ref[...] = dx_acc[...].astype(bf16)

    def finish(k, carry):
        for t in range(n):

            @pl.when(t > z)
            def _():
                rs_up(k, t).wait_send()

            @pl.when(t < z)
            def _():
                rs_down(k, t).wait_send()

            @pl.when(both(t <= z, z < n - 1))
            def _():
                ag_up(k, t).wait_send()

            @pl.when(both(t >= z, z > 0))
            def _():
                ag_down(k, t).wait_send()

        return carry

    lax.fori_loop(0, count, finish, 0)
    for k in range(max(0, count - 2), count):
        dw_copy(k).wait()


def pick_width(units):
    width = min(WIDTH, units)
    while units % width:
        width -= 128
    return width


def grid_call(n, plane, x, weight, act_grad):
    rows, units = act_grad.shape
    depth = weight.shape[0]
    tokens = n * rows
    width = pick_width(units)
    count = units // width
    bf16, f32 = jnp.bfloat16, jnp.float32
    vmem = pl.BlockSpec(memory_space=pltpu.VMEM)
    hbm = pl.BlockSpec(memory_space=pl.ANY)
    chunks = (count, tokens, width)
    dma = pltpu.SemaphoreType.DMA
    sum_rows = tokens // (CHIPS * CORES) if plane else tokens
    scratch = [
        pltpu.VMEM((count, depth, width), bf16),
        pltpu.VMEM(chunks, f32),
        pltpu.VMEM(chunks, bf16),
        pltpu.VMEM(chunks, bf16),
        pltpu.VMEM(chunks, bf16),
        pltpu.VMEM(chunks, bf16),
        pltpu.VMEM((tokens, depth), f32),
        pltpu.VMEM((2, depth, width), bf16),
        pltpu.VMEM((depth, tokens), bf16),
        pltpu.VMEM((rows, units), bf16),
        dma,
        dma((count,)),
        dma((2,)),
    ] + [dma((count, n))] * 6
    if plane:
        part = (rows // CHIPS, x.shape[1])
        scratch += [
            pltpu.VMEM((tokens, depth), bf16),
            pltpu.VMEM((CHIPS,) + part, bf16),
            pltpu.VMEM((n,) + part, bf16),
        ]
        scratch += [pltpu.VMEM((CHIPS, sum_rows, depth), bf16)] * 4
        scratch += [dma((CHIPS,))] * 2 + [dma((n,))] * 2 + [dma((n, CHIPS))] * 4 + [dma((CHIPS,))] * 4
    return pl.pallas_call(
        functools.partial(grid_kernel, n, count, width, rows, LAG, plane),
        out_shape=(
            jax.ShapeDtypeStruct((rows, units), bf16),
            jax.ShapeDtypeStruct((sum_rows, depth), bf16),
            jax.ShapeDtypeStruct((depth, units), bf16),
        ),
        in_specs=[vmem, hbm, hbm],
        out_specs=(vmem, vmem, hbm),
        scratch_shapes=scratch,
        compiler_params=pltpu.CompilerParams(
            collective_id=0, has_side_effects=True, vmem_limit_bytes=60 * 1024 * 1024
        ),
        cost_estimate=pl.CostEstimate(
            flops=6 * tokens * depth * units, bytes_accessed=4 * depth * units, transcendentals=rows * units
        ),
    )(x, weight, act_grad)


def local(n, columns, tokens, weight, act_grad):
    rows, part = tokens.shape
    if n == CHIPS and columns == CHIPS * CORES and rows % (16 * CHIPS) == 0 and part % 128 == 0:
        return grid_call(n, True, tokens, weight, act_grad)
    row_block = lax.all_gather(tokens, "col", axis=1, tiled=True)
    token_cols = lax.all_to_all(row_block, "row", split_axis=1, concat_axis=0, tiled=True)
    activation, partial_grad, weight_grad = grid_call(n, False, token_cols, weight, act_grad)
    input_grad = lax.psum_scatter(partial_grad, "col", scatter_dimension=0, tiled=True)
    return (activation, input_grad, weight_grad)


def solution(mesh):
    placed = (P("row", "col"), P("row", "col"), P("row", "col"))
    return jax.shard_map(
        functools.partial(local, mesh.shape["row"], mesh.shape["col"]),
        mesh=mesh,
        in_specs=placed,
        out_specs=(P("row", "col"), P("col", "row"), P("row", "col")),
        check_vma=False,
    )
```
